128 devices in a mesh: group: 8 (over y_hi, z), member: 16 (over y_lo, x, core).
Axes of the slice: x: 4, y: 4 (y_hi: 2, y_lo: 2; y = y_hi * 2 + y_lo), z: 4, core: 2. Of those that a mesh axis runs over, the one named last changes fastest.
Arguments:
- embeddings: bfloat16 [16, 8192, 1024], P('group', 'member')
- order_rank: int32 [16, 8192], P('group', 'member'), may hold values from 0 to 8191, each once within a row
- lengths: int32 [16], P('group'), may hold values from 1 to 8192, 65536 in all
Outputs:
- highest: float32 [16, 8192], P('group', 'member')
The draws below stay inside these ranges and needn't reach their ends.
Inputs may be any that keep to these rules, and one draw needn't show every extreme that they name: `order_rank`: the ranks of one cluster are distinct.
All inputs are finite; a program needn't handle non-finite values. No bound on the sum of `lengths` on one device may be relied on, other than what follows from the above.
Results may differ from the reference program's by a relative error of at most 0.0003.
Values may be sent and summed in bfloat16 or wider, within the bound.
A program may use at most 128 MiB of HBM per device.

```python
import math
import jax
import jax.numpy as jnp
import numpy as np
from jax import lax

D = 1024
SLOT_DEV = 512
CAP = 8192
CLUSTERS = 16


def draw_embeddings(key, part):
    key = jax.random.fold_in(key, 11)
    keys_all = jax.random.split(key, 6)
    shared = jax.random.normal(keys_all[0], (D,), jnp.float32) * 3.0
    centroid = jax.random.normal(keys_all[1], (CLUSTERS, 1, D), jnp.float32)
    sources = jax.random.normal(keys_all[2], (CLUSTERS, CAP // 4, D), jnp.float32)
    picks = jax.random.randint(keys_all[3], (CLUSTERS, CAP), 0, CAP // 4)
    based = jnp.take_along_axis(sources, picks[:, :, None], axis=1)
    weights = jax.random.uniform(keys_all[4], (CLUSTERS, CAP, 1), jnp.float32, 0.3, 1.5)
    noise = jax.random.normal(keys_all[5], (CLUSTERS, CAP, D), jnp.float32) * 0.6
    return (shared + centroid + weights * based + noise).astype(jnp.bfloat16)


def profile(number_of, total, reach, skew):
    weights = [(1 << 20) // math.isqrt(standing ** skew) + 1 for standing in range(2, number_of + 1)]
    rest, counts = total - reach - (number_of - 1), [1] * (number_of - 1)
    while rest > 0:
        free = [i for i in range(number_of - 1) if counts[i] < reach]
        pool, remaining = sum([weights[i] for i in free]), rest
        for i in free:
            extra = min(reach - counts[i], max(1, remaining * weights[i] // pool), rest)
            counts[i] = counts[i] + extra
            rest = rest - extra
    return np.array([reach] + counts)


def uneven_parts(key, number_of, total, limit, lean):
    if number_of == 2:
        one = jax.random.randint(key, (), max(1, total - limit), min(limit, total - 1) + 1)
        return jnp.stack([one, total - one])
    sizes = jnp.asarray(profile(number_of, total, limit, lean), jnp.int32)
    twos = (number_of - 1) // 2
    donor, sink = sizes[1:1 + 2 * twos:2], sizes[2:2 + 2 * twos:2]
    margin = jnp.minimum(donor - 1, limit - sink)
    moved = jax.random.randint(jax.random.fold_in(key, 1), (twos,), 0, 1 << 20) % (margin + 1)
    sizes = sizes.at[1:1 + 2 * twos:2].set(donor - moved).at[2:2 + 2 * twos:2].set(sink + moved)
    return sizes[jax.random.permutation(jax.random.fold_in(key, 2), number_of)]


def setup_inputs(seed: int = 0) -> dict:
    splits = jax.random.split(jax.random.key(seed), 4)
    return {
        "embeddings": draw_embeddings(jax.random.fold_in(splits[3], 71), 0),
        "order_rank": jax.vmap(lambda own: jax.random.permutation(own, CAP))(jax.random.split(splits[1], CLUSTERS)).reshape((CLUSTERS, CAP)).astype(jnp.int32),
        "lengths": uneven_parts(splits[2], CLUSTERS, CLUSTERS * CAP // 2, CAP, 2).astype(jnp.int32),
    }


def cluster_scan(normed_rows, rank_row, length_one):
    slots = jnp.arange(CAP, dtype=jnp.int32)
    col_live = slots < length_one
    blocks = normed_rows.reshape(CAP // SLOT_DEV, SLOT_DEV, D)
    rank_blocks = rank_row.reshape(CAP // SLOT_DEV, SLOT_DEV)
    live_blocks = col_live.reshape(CAP // SLOT_DEV, SLOT_DEV)

    def one_block(parts):
        rows, row_rank, row_live = parts
        cosines = jnp.dot(rows, normed_rows.T, preferred_element_type=jnp.float32)
        allowed = col_live[None, :] & (rank_row[None, :] < row_rank[:, None])
        largest = lax.optimization_barrier(jnp.max(jnp.where(allowed, cosines, -1.0), axis=1))
        return jnp.where(row_live, largest, -1.0)
    return lax.map(one_block, (blocks, rank_blocks, live_blocks)).reshape(CAP)

def reference(embeddings, order_rank, lengths):
    slots = jnp.arange(CAP, dtype=jnp.int32)
    live = slots[None, :] < lengths[:, None]
    values = embeddings.astype(jnp.float32)
    summed = lax.optimization_barrier(jnp.sum(jnp.where(live[:, :, None], values, 0.0), axis=(0, 1)))
    counted = jnp.sum(live.astype(jnp.float32))
    center = summed / counted
    shifted = values - center
    normed = (shifted * lax.rsqrt(lax.optimization_barrier(jnp.sum(shifted * shifted, axis=-1, keepdims=True)) + 1e-06)).astype(jnp.bfloat16)
    return lax.map(lambda parts: cluster_scan(parts[0], parts[1], parts[2]), (normed, order_rank, lengths))
```

```python
import functools

import jax
import jax.numpy as jnp
from jax import lax
from jax.experimental import pallas as pl
from jax.experimental.pallas import tpu as pltpu
from jax.sharding import PartitionSpec as P

MESH = pl.DeviceIdType.MESH
UNIT = 128
PER = 4
STEPS = 6
LP, LQ, LR = 4, 10, 16
OTHER = 22
NO_RANK = 1e9
FILL, BULK = 8, 12
WIDE = 4
NONE = -1


def needed(role):
    own, q, r = (0, 2), (LQ, LQ + 2, LQ + 4), (LR, LR + 2, LR + 4)
    p = (LP + 2, LP + 4) if role == 2 else (LP, LP + 2)
    columns = lambda firsts: [u + i for u in firsts for i in range(2)]
    jobs = []
    if role == 2:
        jobs += [(u, v) for u in own + r[:2] for v in columns(q)]
        jobs += [(u, v) for u in p for v in columns(q[2:])] + [(u, v) for u in q[:2] for v in columns(p)]
        jobs += [(u, v) for u in q for v in columns(q) if v >= u]
        jobs += [(u, v) for u in own for v in columns(own) if v >= u]
        jobs += [(u, v) for u in own for v in columns(r[:2])]
        jobs += [(r[0], v) for v in columns(r[:2])]
    else:
        jobs += [(u, v) for u in own + p for v in columns(q + r)]
        if role == 0:
            for a in range(3):
                for b in range(3):
                    jobs += [(q[a], v) for v in columns([r[b]])] if b >= a else [(r[b], v) for v in columns([q[a]])]
        else:
            jobs += [(u, v) for u in own + p for v in columns(own + p) if v >= u]
            jobs += [(u, v) for u in q[:2] for v in columns(r[:2])]
    return jobs


def jobs_of(role):
    def there(unit):
        return 0 if unit < LP else (unit - LP) % STEPS + 1

    todo = sorted(needed(role), key=lambda job: max(there(job[0] + 1), there(job[1])))
    ready = lambda job: max(there(job[0] + 1), there(job[1]))
    plan, at = [], 0
    for stage in range(STEPS + 1):
        for limit, cap in ((stage - 1, FILL), (stage, BULK)):
            if stage == STEPS:
                cap = len(todo)
            take = []
            while at < len(todo) and ready(todo[at]) <= limit and len(take) < cap:
                take.append(todo[at])
                at += 1
            plan.append(take)
    return plan


def pick(index, values):
    out = jnp.int32(values[0])
    for i in range(1, len(values)):
        out = jnp.where(index == i, values[i], out)
    return out


def kernel(
    groups, lengths_hbm, emb, order_hbm, out, lengths, order, raw, norm, cranks, rranks, rowacc, colacc, sums, totals, ret, back, center,
    load_sem, raw_send, raw_recv, core_send, core_recv, sum_send, sum_recv, total_send, total_recv, ret_send, ret_recv,
):
    group, member = lax.axis_index("group"), lax.axis_index("member")
    core, x, y = member % 2, (member // 2) % 4, member // 8
    role = (x + 2 * y) % 4
    is_m = jnp.where(role == 3, 1, 0)
    mine = y + is_m * (1 - 2 * y)
    chip = 4 * y + x
    sibling = {"member": 2 * chip + 1 - core}

    def actual(c):
        cx, cy = c % 4, c // 4
        return (cx + 2 * mine) % 4 + 4 * (cy + mine * (1 - 2 * cy))

    xp, xm, yy = 4 * y + (x + 1) % 4, 4 * y + (x + 3) % 4, 4 * (1 - y) + x
    neighbour = [
        jnp.where(role == 0, xp, jnp.where(role == 3, yy, xm)),
        jnp.where((role == 1) | (role == 2), xp, xm),
        jnp.where(role == 3, xp, yy),
    ]
    bases = (LP, LQ, LR)
    landing = [
        pick(role, (LP, LP, LQ, LR)),
        pick(role, (LR, LP, LQ, LQ)),
        pick(role, (LR, LP, LR, LQ)),
    ]
    late_pair = role >= 2

    small = [
        pltpu.make_async_copy(lengths_hbm, lengths, load_sem.at[2]),
        pltpu.make_async_copy(order_hbm, order, load_sem.at[3]),
    ]
    for cp in small:
        cp.start()
    loads = []
    for i, (cluster, first) in enumerate(((mine, 0), (1 - mine, OTHER))):
        loads.append(pltpu.make_async_copy(emb.at[cluster], raw.at[pl.ds(first, PER)], load_sem.at[i]))
        loads[-1].start()
    barrier = pltpu.get_barrier_semaphore()
    for i in range(1, 16):
        pl.semaphore_signal(barrier, inc=1, device_id={"member": (member + i) % 16}, device_id_type=MESH)
    for i in range(1, groups):
        pl.semaphore_signal(barrier, inc=1, device_id={"group": (group + i) % groups}, device_id_type=MESH)

    rowacc[...] = jnp.full(rowacc.shape, -1.0, jnp.float32)
    colacc[...] = jnp.full(colacc.shape, -1.0, jnp.float32)
    ret[...] = jnp.full(ret.shape, -1.0, jnp.float32)
    back[...] = jnp.full(back.shape, -1.0, jnp.float32)

    for cp in small:
        cp.wait()
    first_slot = member * (PER * UNIT)
    lane = lax.broadcasted_iota(jnp.int32, (1, UNIT), 1)
    own_ranks, own_live = [], []
    for c in range(2):
        for i in range(PER):
            is_live = first_slot + i * UNIT + lane < lengths[c]
            own_live.append(is_live)
            own = order[c : c + 1, i * UNIT : (i + 1) * UNIT].astype(jnp.float32)
            own_ranks.append(jnp.where(is_live, own, NO_RANK))
    sums[member, 16:24, :] = jnp.concatenate(own_ranks, axis=0)

    for cp in loads:
        cp.wait()
    row = lax.broadcasted_iota(jnp.int32, (UNIT, 1), 0)

    def add_unit(i, carry):
        total, count = carry
        other = i // PER
        cluster = mine + other * (1 - 2 * mine)
        at = i % PER
        is_live = first_slot + at * UNIT + row < lengths[cluster]
        values = jnp.where(is_live, raw[at + other * OTHER].astype(jnp.float32), 0.0)
        total = total + jnp.sum(values.reshape(UNIT // 8, 8, -1), axis=0)
        count = count + jnp.sum(is_live.astype(jnp.float32), axis=0, keepdims=True)
        return total, count

    total, count = lax.fori_loop(0, 2 * PER, add_unit, (jnp.zeros((8, 1024), jnp.float32), jnp.zeros((1, 1), jnp.float32)))
    total = jnp.sum(total, axis=0, keepdims=True)
    rows_out = [total[:, 128 * i : 128 * (i + 1)] for i in range(8)]
    rows_out += [jnp.broadcast_to(count, (1, 128))] + [jnp.zeros((7, 128), jnp.float32)]
    sums[member, 0:16, :] = jnp.concatenate(rows_out, axis=0)

    pl.semaphore_wait(barrier, 15 + groups - 1)

    def to_member(buffer, send, recv, i):
        return pltpu.make_async_remote_copy(
            src_ref=buffer.at[member], dst_ref=buffer.at[member], send_sem=send.at[i], recv_sem=recv.at[member],
            device_id={"member": (member + i) % 16}, device_id_type=MESH,
        )

    def from_member(buffer, send, recv, i):
        source = (member + 16 - i) % 16
        return pltpu.make_async_remote_copy(
            src_ref=buffer.at[source], dst_ref=buffer.at[source], send_sem=send.at[i], recv_sem=recv.at[source],
            device_id={"member": (member + i) % 16}, device_id_type=MESH,
        )

    for i in range(1, 16):
        to_member(sums, sum_send, sum_recv, i).start()

    def source_of(link, s):
        if link == 0:
            return s if s < 4 else LR + s - 4
        by_c = (OTHER + (2 if link == 1 else 0) + s) if s < 2 else ((LR if link == 1 else LQ) + s - 2)
        by_h = OTHER + ((s + 2) % 4 if link == 1 else s % 4)
        by_lm = OTHER + s if s < 4 else LP + s - 4
        return pick(role, (by_h, by_c, by_lm, by_lm))

    def goes(link, s):
        if s < 4:
            return None
        return late_pair if link == 0 else role != 0

    def outgoing(link, s):
        return pltpu.make_async_remote_copy(
            src_ref=raw.at[source_of(link, s)], dst_ref=raw.at[landing[link] + s],
            send_sem=raw_send.at[link, s], recv_sem=raw_recv.at[landing[link] - LP + s],
            device_id={"member": 2 * neighbour[link] + core}, device_id_type=MESH,
        )

    def arriving(link, s):
        unit = bases[link] + s
        return pltpu.make_async_remote_copy(
            src_ref=raw.at[unit], dst_ref=raw.at[unit], send_sem=raw_send.at[link, s], recv_sem=raw_recv.at[unit - LP],
            device_id={"member": 2 * neighbour[link] + core}, device_id_type=MESH,
        )

    def comes(link, s):
        if s < 4 or link == 1:
            return None
        return late_pair if link == 0 else jnp.logical_not(late_pair)

    def guarded(condition, do):
        if condition is None:
            do()
        else:
            pl.when(condition)(do)

    is_c = role == 1

    def send_step(s, everyone):
        for link in range(3):
            condition = None if everyone or link == 0 else jnp.logical_not(is_c)
            guarded(condition, lambda link=link: outgoing(link, s).start())

    def forward(s):
        if s == 0:
            send_step(1, True)
        if s + 2 < 4:
            send_step(s + 2, False)
        if s in (2, 3):

            @pl.when(late_pair)
            def _():
                for link in range(3):
                    outgoing(link, s + 2).start()

        if s < 4:

            @pl.when(is_c)
            def _():
                for link in (1, 2):
                    outgoing(link, s + 2).start()

    def arrive(s):
        for link in range(3):
            guarded(comes(link, s), lambda link=link: arriving(link, s).wait_recv())
        forward(s)

    send_step(0, True)

    for i in range(1, 16):
        from_member(sums, sum_send, sum_recv, i).wait_recv()
    totals[group] = jnp.sum(sums[:, 0:16, :], axis=0)

    def across(i, source):
        at = (group + groups - i) % groups if source else group
        return pltpu.make_async_remote_copy(
            src_ref=totals.at[at], dst_ref=totals.at[at], send_sem=total_send.at[i], recv_sem=total_recv.at[at],
            device_id={"group": (group + i) % groups}, device_id_type=MESH,
        )

    for i in range(1, groups):
        across(i, False).start()

    def owner_of(link, s):
        if link == 0:
            return actual(pick(role, (1, 0, 5, 2))), (s - 2 * jnp.where(late_pair, 1, 0))
        if link == 1:
            if s < 4:
                return actual(pick(role, (3, 2, 3, 4))), s
            return actual(pick(role, (7, 6, 7, 7))), s - 4 + 2 * is_m
        if s < 4:
            return actual(pick(role, (4, 5, 6, 6))), (s + 2 * is_m) % 4
        return actual(pick(role, (7, 6, 7, 7))), s - 2

    def set_ranks(unit, owner, at):
        line = 4 * mine + at
        both = [sums[2 * owner + j, pl.ds(16 + line, 1), :] for j in range(2)]
        cranks[unit] = jnp.concatenate(both, axis=1)
        own = sums[2 * owner + core, pl.ds(16 + line, 1), :]
        rranks[unit] = jnp.broadcast_to(own, (UNIT, UNIT)).T

    arrive(0)
    for i in range(PER):
        set_ranks(i, chip, i)
    for link in range(3):
        for s in range(STEPS):
            unit = bases[link] + s

            def one(link=link, s=s, unit=unit):
                set_ranks(unit, *owner_of(link, s))

            condition = comes(link, s)
            if link == 0 and s < 2:
                condition = jnp.logical_not(late_pair)
            guarded(condition, one)

    for i in range(1, groups):
        across(i, True).wait_recv()
    whole = jnp.sum(totals[...], axis=0)
    mean = whole[0:8] / whole[8:9]
    center[...] = jnp.concatenate([mean[i : i + 1] for i in range(8)], axis=1)

    half = pl.ds(pl.multiple_of(core * UNIT, UNIT), UNIT)
    theirs = pl.ds(pl.multiple_of((1 - core) * UNIT, UNIT), UNIT)

    def normalise(unit):
        shifted = raw[unit].astype(jnp.float32) - center[...]
        scale = lax.rsqrt(jnp.sum(shifted * shifted, axis=-1, keepdims=True) + 1e-06)
        norm[unit, half, :] = (shifted * scale).astype(jnp.bfloat16)

    def exchange(unit, rows):
        return pltpu.make_async_remote_copy(
            src_ref=norm.at[unit, rows], dst_ref=norm.at[unit, rows], send_sem=core_send.at[unit], recv_sem=core_recv.at[unit],
            device_id=sibling, device_id_type=MESH,
        )

    def prepare(unit):
        normalise(unit)
        exchange(unit, half).start()

    def pair(u, v):
        rows = norm[pl.ds(u, 2), half, :].reshape(2 * UNIT, 1024)
        cosines = lax.dot_general(rows, norm[v], (((1,), (1,)), ((), ())), preferred_element_type=jnp.float32)
        own = rranks[pl.ds(u, 2)].reshape(2 * UNIT, UNIT)
        best_rows = rowacc[pl.ds(u, 2)].reshape(2 * UNIT, UNIT)
        for h in range(2):
            at = slice(UNIT * h, UNIT * (h + 1))
            part, other = cosines[:, at], cranks[v, :, at]
            best_rows = jnp.maximum(best_rows, jnp.where(other < own, part, -1.0))
            up = jnp.where(own < other, part, -1.0)
            colacc[v, :, at] = jnp.maximum(colacc[v, :, at], jnp.max(up.reshape(2 * UNIT // 8, 8, UNIT), axis=0))
        rowacc[pl.ds(u, 2)] = best_rows.reshape(2, UNIT, UNIT)

    plans = [jobs_of(r) for r in range(3)]

    def run_jobs(part):
        lists = [plan[part] + plan[part][-1:] * (-len(plan[part]) % WIDE) for plan in plans]
        lists.append(lists[2])
        longest = max(len(jobs) for jobs in lists)
        if not longest:
            return
        codes = []
        for j in range(longest):
            at = [jobs[j][0] * 32 + jobs[j][1] if j < len(jobs) else 0 for jobs in lists]
            codes.append(pick(role, at))

        def body(j, _):
            for k in range(WIDE):
                code = codes[k]
                for i in range(1, longest // WIDE):
                    code = jnp.where(j == i, codes[WIDE * i + k], code)
                pair(code // 32, code % 32)
            return 0

        lax.fori_loop(0, pick(role, [len(jobs) // WIDE for jobs in lists]), body, 0)

    def held(link, s):
        if link == 0 and s < 2:
            return jnp.logical_not(late_pair)
        return comes(link, s)

    def own_unit(unit, _):
        prepare(unit)
        return 0

    lax.fori_loop(0, PER, own_unit, 0)
    arrive(1)
    for i in range(PER):
        exchange(i, theirs).wait_recv()
    run_jobs(1)
    for s in range(STEPS):
        if s > 1:
            arrive(s)
        for link in range(3):
            guarded(held(link, s), lambda link=link: prepare(bases[link] + s))
        run_jobs(2 * s + 2)
        for link in range(3):
            guarded(held(link, s), lambda link=link: exchange(bases[link] + s, theirs).wait_recv())
        run_jobs(2 * s + 3)

    def finish(unit, slot, at):
        best = jnp.max(colacc[unit], axis=0, keepdims=True)
        across_lanes = jnp.max(rowacc[unit].T, axis=0, keepdims=True)
        for j in range(2):
            part = best[:, UNIT * j : UNIT * (j + 1)]
            ret[slot, j, pl.ds(at, 1), :] = jnp.where(core == j, jnp.maximum(part, across_lanes), part)

    for link in range(3):
        for s in range(STEPS):
            slot = 1 + link if s < 4 or link == 0 else 4
            guarded(held(link, s), lambda link=link, s=s, slot=slot: finish(bases[link] + s, slot, owner_of(link, s)[1]))
    owners = [owner_of(0, 2)[0], owner_of(1, 0)[0], owner_of(2, 0)[0], owner_of(1, 4)[0]]

    def give(slot, j):
        return pltpu.make_async_remote_copy(
            src_ref=ret.at[slot, j], dst_ref=back.at[2 * chip + core], send_sem=ret_send.at[slot, j], recv_sem=ret_recv.at[2 * chip + core],
            device_id={"member": 2 * owners[slot - 1] + j}, device_id_type=MESH,
        )

    for slot in range(1, 5):
        for j in range(2):
            give(slot, j).start()
    for i in range(PER):
        finish(i, 0, i)
    to_sibling = pltpu.make_async_remote_copy(
        src_ref=ret.at[0, 1 - core], dst_ref=back.at[member], send_sem=ret_send.at[0, 0], recv_sem=ret_recv.at[member],
        device_id=sibling, device_id_type=MESH,
    )
    to_sibling.start()

    other_of = lambda c: (c % 4 + 2) % 4 + 4 * (1 - c // 4)
    givers = [
        actual(pick(role, (1, 0, 1, 1))),
        jnp.where(late_pair, actual(pick(role, (5, 5, 5, 2))), other_of(actual(pick(role, (1, 0, 0, 0))))),
        other_of(actual(pick(role, (2, 2, 0, 0)))),
        other_of(actual(pick(role, (5, 5, 5, 2)))),
    ]

    def take(source):
        return pltpu.make_async_remote_copy(
            src_ref=back.at[source], dst_ref=back.at[source], send_sem=ret_send.at[0, 1], recv_sem=ret_recv.at[source],
            device_id=sibling, device_id_type=MESH,
        )

    take(2 * chip + 1 - core).wait_recv()
    for giver in givers:
        for j in range(2):
            take(2 * giver + j).wait_recv()
    computes = lambda c: (c // 4) if c != 3 and c != 5 else 1 - c // 4
    for c in range(2):
        best = jnp.maximum(jnp.full((8, UNIT), -1.0, jnp.float32), jnp.where(mine == c, ret[0, core], -1.0))
        for source in range(16):
            if computes(source // 2) == c:
                best = jnp.maximum(best, back[source])
        for i in range(PER):
            out[c : c + 1, i * UNIT : (i + 1) * UNIT] = jnp.where(own_live[c * PER + i], best[i : i + 1], -1.0)

    for i in range(1, 16):
        to_member(sums, sum_send, sum_recv, i).wait_send()
    for i in range(1, groups):
        across(i, False).wait_send()
    for s in range(STEPS):
        for link in range(3):
            guarded(goes(link, s), lambda link=link: outgoing(link, s).wait_send())
    for i in range(PER):
        exchange(i, half).wait_send()
    for s in range(STEPS):
        for link in range(3):
            guarded(held(link, s), lambda link=link: exchange(bases[link] + s, half).wait_send())
    for slot in range(1, 5):
        for j in range(2):
            give(slot, j).wait_send()
    to_sibling.wait_send()


def solution(mesh):
    groups = mesh.shape["group"]
    units = LR + STEPS

    def local(embeddings, order_rank, lengths):
        d = embeddings.shape[-1]
        f32, dma = jnp.float32, pltpu.SemaphoreType.DMA
        return pl.pallas_call(
            functools.partial(kernel, groups),
            out_shape=jax.ShapeDtypeStruct(order_rank.shape, f32),
            in_specs=[
                pl.BlockSpec(memory_space=pl.ANY),
                pl.BlockSpec(memory_space=pl.ANY),
                pl.BlockSpec(memory_space=pl.ANY),
            ],
            out_specs=pl.BlockSpec(memory_space=pltpu.VMEM),
            scratch_shapes=[
                pltpu.SMEM(lengths.shape, jnp.int32),
                pltpu.VMEM(order_rank.shape, jnp.int32),
                pltpu.VMEM((OTHER + PER, UNIT, d), jnp.bfloat16),
                pltpu.VMEM((units, 2 * UNIT, d), jnp.bfloat16),
                pltpu.VMEM((units, 1, 2 * UNIT), f32),
                pltpu.VMEM((units, UNIT, UNIT), f32),
                pltpu.VMEM((units, UNIT, UNIT), f32),
                pltpu.VMEM((units, 8, 2 * UNIT), f32),
                pltpu.VMEM((16, 24, UNIT), f32),
                pltpu.VMEM((groups, 16, UNIT), f32),
                pltpu.VMEM((5, 2, 8, UNIT), f32),
                pltpu.VMEM((16, 8, UNIT), f32),
                pltpu.VMEM((1, d), f32),
                dma((4,)),
                dma((3, STEPS)),
                dma((3 * STEPS,)),
                dma((units,)),
                dma((units,)),
                dma((16,)),
                dma((16,)),
                dma((groups,)),
                dma((groups,)),
                dma((5, 2)),
                dma((16,)),
            ],
            compiler_params=pltpu.CompilerParams(collective_id=0, has_side_effects=True, vmem_limit_bytes=60 * 1024 * 1024),
            cost_estimate=pl.CostEstimate(flops=10_000_000_000, bytes_accessed=4_000_000, transcendentals=10_000),
        )(lengths, embeddings.reshape(2, PER, UNIT, d), order_rank)

    placed = (P("group", "member", None), P("group", "member"), P("group"))
    return jax.shard_map(local, mesh=mesh, in_specs=placed, out_specs=P("group", "member"), check_vma=False)
```

```python
import jax
import jax.numpy as jnp
from jax import lax
from jax.experimental import pallas as pl
from jax.experimental.pallas import tpu as pltpu
from jax.sharding import PartitionSpec as P

MESH = pl.DeviceIdType.MESH
UNIT = 128
PER = 4
STEPS = 6
LP, LQ, LR = 4, 10, 16
OTHER = 22
NO_RANK = 1e9
AHEAD = 2
LEAVE = 8
WIDE = 4
NONE = -1


def needed(role):
    own, q, r = (0, 2), (LQ, LQ + 2, LQ + 4), (LR, LR + 2, LR + 4)
    p = (LP + 2, LP + 4) if role == 2 else (LP, LP + 2)
    columns = lambda firsts: [u + i for u in firsts for i in range(2)]
    jobs = []
    if role == 2:
        jobs += [(u, v) for u in own + r[:2] for v in columns(q)]
        jobs += [(u, v) for u in p for v in columns(q[2:])] + [(u, v) for u in q[:2] for v in columns(p)]
        jobs += [(u, v) for u in q for v in columns(q) if v >= u]
        jobs += [(u, v) for u in own for v in columns(own) if v >= u]
        jobs += [(u, v) for u in own for v in columns(r[:2])]
        jobs += [(r[0], v) for v in columns(r[:2])]
    else:
        jobs += [(u, v) for u in own + p for v in columns(q + r)]
        if role == 0:
            for a in range(3):
                for b in range(3):
                    jobs += [(q[a], v) for v in columns([r[b]])] if b >= a else [(r[b], v) for v in columns([q[a]])]
        else:
            jobs += [(u, v) for u in own + p for v in columns(own + p) if v >= u]
            jobs += [(u, v) for u in q[:2] for v in columns(r[:2])]
    return jobs


def jobs_of(role):
    def there(unit):
        return 0 if unit < LP else (unit - LP) % STEPS + 1

    ready = lambda job: max(there(job[0] + 1), there(job[1]))
    todo = sorted(needed(role), key=ready)
    plan, at = [], 0

    def take(limit, leave):
        nonlocal at
        able = sum(ready(job) <= limit for job in todo)
        until = max(at, able - leave)
        plan.append(todo[at:until])
        at = until

    take(0, 0)
    for s in range(AHEAD):
        take(s + 1, LEAVE if s == AHEAD - 1 else 0)
    for s in range(AHEAD, STEPS):
        take(s, 0)
        take(s + 1, LEAVE if s < STEPS - 1 else 0)
    return plan


def pick(index, values):
    out = jnp.int32(values[0])
    for i in range(1, len(values)):
        out = jnp.where(index == i, values[i], out)
    return out


def kernel(
    lengths_hbm, emb, order_hbm, out, lengths, order, raw, norm, cranks, rranks, rowacc, colacc, sums, parts, tiles, ret, back, center,
    load_sem, raw_send, raw_recv, core_send, core_recv, sum_send, sum_recv, part_send, part_recv, tile_send, tile_recv, ret_send, ret_recv,
):
    group, member = lax.axis_index("group"), lax.axis_index("member")
    core, x, y = member % 2, (member // 2) % 4, member // 8
    role = (x + 2 * y) % 4
    is_m = jnp.where(role == 3, 1, 0)
    mine = y + is_m * (1 - 2 * y)
    chip = 4 * y + x
    sibling = {"member": 2 * chip + 1 - core}

    def actual(c):
        cx, cy = c % 4, c // 4
        return (cx + 2 * mine) % 4 + 4 * (cy + mine * (1 - 2 * cy))

    xp, xm, yy = 4 * y + (x + 1) % 4, 4 * y + (x + 3) % 4, 4 * (1 - y) + x
    neighbour = [
        jnp.where(role == 0, xp, jnp.where(role == 3, yy, xm)),
        jnp.where((role == 1) | (role == 2), xp, xm),
        jnp.where(role == 3, xp, yy),
    ]
    bases = (LP, LQ, LR)
    landing = [
        pick(role, (LP, LP, LQ, LR)),
        pick(role, (LR, LP, LQ, LQ)),
        pick(role, (LR, LP, LR, LQ)),
    ]
    late_pair = role >= 2
    is_c = role == 1

    small = [
        pltpu.make_async_copy(lengths_hbm, lengths, load_sem.at[2]),
        pltpu.make_async_copy(order_hbm, order, load_sem.at[3]),
    ]
    for cp in small:
        cp.start()
    loads = []
    for i, (cluster, first) in enumerate(((mine, 0), (1 - mine, OTHER))):
        loads.append(pltpu.make_async_copy(emb.at[cluster], raw.at[pl.ds(first, PER)], load_sem.at[i]))
        loads[-1].start()
    barrier = pltpu.get_barrier_semaphore()
    z, wide_y = group % 4, 2 * (group // 4) + y

    def along(axis, i):
        if axis == 0:
            return {"group": 4 * (group // 4) + (z + i) % 4, "member": member}
        if axis == 1:
            to = (wide_y + i) % 4
            return {"group": 4 * (to // 2) + z, "member": 8 * (to % 2) + 2 * x + core}
        return {"group": group, "member": 8 * y + 2 * ((x + i) % 4) + core}

    for axis in range(3):
        for i in range(1, 4):
            pl.semaphore_signal(barrier, inc=1, device_id=along(axis, i), device_id_type=MESH)
    pl.semaphore_signal(barrier, inc=1, device_id=sibling, device_id_type=MESH)

    ret[...] = jnp.full(ret.shape, -1.0, jnp.float32)
    back[...] = jnp.full(back.shape, -1.0, jnp.float32)

    for cp in small:
        cp.wait()
    first_slot = member * (PER * UNIT)
    lane = lax.broadcasted_iota(jnp.int32, (1, UNIT), 1)
    own_ranks, own_live = [], []
    for c in range(2):
        for i in range(PER):
            is_live = first_slot + i * UNIT + lane < lengths[c]
            own_live.append(is_live)
            own = order[c : c + 1, i * UNIT : (i + 1) * UNIT].astype(jnp.float32)
            own_ranks.append(jnp.where(is_live, own, NO_RANK))
    by_cluster = [jnp.concatenate(own_ranks[PER * c : PER * (c + 1)], axis=0) for c in range(2)]
    first = mine == 0
    sums[core, 16:24, :] = jnp.concatenate(
        [jnp.where(first, by_cluster[0], by_cluster[1]), jnp.where(first, by_cluster[1], by_cluster[0])], axis=0
    )

    for cp in loads:
        cp.wait()
    row = lax.broadcasted_iota(jnp.int32, (UNIT, 1), 0)

    def add_unit(i, carry):
        total, count = carry
        other = i // PER
        cluster = mine + other * (1 - 2 * mine)
        at = i % PER
        is_live = first_slot + at * UNIT + row < lengths[cluster]
        values = jnp.where(is_live, raw[at + other * OTHER].astype(jnp.float32), 0.0)
        total = total + jnp.sum(values.reshape(UNIT // 8, 8, -1), axis=0)
        count = count + jnp.sum(is_live.astype(jnp.float32), axis=0, keepdims=True)
        return total, count

    total, count = lax.fori_loop(0, 2 * PER, add_unit, (jnp.zeros((8, 1024), jnp.float32), jnp.zeros((1, 1), jnp.float32)))
    total = jnp.sum(total, axis=0, keepdims=True)
    rows_out = [total[:, 128 * i : 128 * (i + 1)] for i in range(8)]
    rows_out += [jnp.broadcast_to(count, (1, 128))] + [jnp.zeros((7, 128), jnp.float32)]
    sums[core, 0:16, :] = jnp.concatenate(rows_out, axis=0)

    pl.semaphore_wait(barrier, 10)

    def with_sibling(slot):
        return pltpu.make_async_remote_copy(
            src_ref=sums.at[slot], dst_ref=sums.at[slot], send_sem=sum_send.at[0], recv_sem=sum_recv.at[0],
            device_id=sibling, device_id_type=MESH,
        )

    with_sibling(core).start()

    def source_of(link, s):
        if link == 0:
            return s if s < 4 else LR + s - 4
        by_c = (OTHER + (2 if link == 1 else 0) + s) if s < 2 else ((LR if link == 1 else LQ) + s - 2)
        by_h = OTHER + ((s + 2) % 4 if link == 1 else s % 4)
        by_lm = OTHER + s if s < 4 else LP + s - 4
        return pick(role, (by_h, by_c, by_lm, by_lm))

    def goes(link, s):
        if s < 4:
            return None
        return late_pair if link == 0 else role != 0

    def outgoing(link, s):
        return pltpu.make_async_remote_copy(
            src_ref=raw.at[source_of(link, s)], dst_ref=raw.at[landing[link] + s],
            send_sem=raw_send.at[link, s], recv_sem=raw_recv.at[landing[link] - LP + s],
            device_id={"member": 2 * neighbour[link] + core}, device_id_type=MESH,
        )

    def arriving(link, s):
        unit = bases[link] + s
        return pltpu.make_async_remote_copy(
            src_ref=raw.at[unit], dst_ref=raw.at[unit], send_sem=raw_send.at[link, s], recv_sem=raw_recv.at[unit - LP],
            device_id={"member": 2 * neighbour[link] + core}, device_id_type=MESH,
        )

    def comes(link, s):
        if s < 4 or link == 1:
            return None
        return late_pair if link == 0 else jnp.logical_not(late_pair)

    def guarded(condition, do):
        if condition is None:
            do()
        else:
            pl.when(condition)(do)

    def held(link, s):
        if link == 0 and s < 2:
            return jnp.logical_not(late_pair)
        return comes(link, s)

    def send_step(s, everyone):
        for link in range(3):
            condition = None if everyone or link == 0 else jnp.logical_not(is_c)
            guarded(condition, lambda link=link: outgoing(link, s).start())

    def forward(s):
        if s in (2, 3):

            @pl.when(late_pair)
            def _():
                for link in range(3):
                    outgoing(link, s + 2).start()

        if s < 4:

            @pl.when(is_c)
            def _():
                for link in (1, 2):
                    outgoing(link, s + 2).start()

    def arrive(s):
        for link in range(3):
            guarded(comes(link, s), lambda link=link: arriving(link, s).wait_recv())
        forward(s)

    send_step(0, True)
    rowacc[...] = jnp.full(rowacc.shape, -1.0, jnp.float32)
    colacc[...] = jnp.full(colacc.shape, -1.0, jnp.float32)

    with_sibling(1 - core).wait_recv()
    place = (z, wide_y, x)

    def part(axis, i, source):
        at = (place[axis] + 4 - i) % 4 if source else place[axis]
        return pltpu.make_async_remote_copy(
            src_ref=parts.at[axis, at], dst_ref=parts.at[axis, at], send_sem=part_send.at[axis, i], recv_sem=part_recv.at[axis, at],
            device_id=along(axis, i), device_id_type=MESH,
        )

    def spread(axis, value):
        parts[axis, place[axis]] = value
        for i in range(1, 4):
            part(axis, i, False).start()

    def gathered(axis):
        for i in range(1, 4):
            part(axis, i, True).wait_recv()
        return (parts[axis, 0] + parts[axis, 1]) + (parts[axis, 2] + parts[axis, 3])

    spread(0, sums[0, 0:16, :] + sums[1, 0:16, :])

    for i in range(2):
        lines = slice(16 + 4 * i, 20 + 4 * i)
        tiles[i] = jnp.concatenate([sums[0, lines, :], sums[1, lines, :]], axis=0)
    far_link = [pick(role, (0, 0, 1, 2)), pick(role, (2, 0, 1, 1)), pick(role, (2, 0, 2, 1))]

    def give_tile(link, again):
        if not again:
            source = 0 if link == 0 else 1
        elif link == 0:
            source = 6
        else:
            source = jnp.where(is_c, 6 if link == 1 else 4, 2)
        landed = 2 + 2 * far_link[link] + again
        return pltpu.make_async_remote_copy(
            src_ref=tiles.at[source], dst_ref=tiles.at[landed], send_sem=tile_send.at[link, again], recv_sem=tile_recv.at[landed],
            device_id={"member": 2 * neighbour[link] + core}, device_id_type=MESH,
        )

    def take_tile(link, again):
        at = 2 + 2 * link + again
        return pltpu.make_async_remote_copy(
            src_ref=tiles.at[at], dst_ref=tiles.at[at], send_sem=tile_send.at[link, again], recv_sem=tile_recv.at[at],
            device_id={"member": 2 * neighbour[link] + core}, device_id_type=MESH,
        )

    for link in range(3):
        give_tile(link, 0).start()

    spread(1, gathered(0))
    send_step(1, True)
    for link in range(3):
        take_tile(link, 0).wait_recv()
    for link in range(3):
        guarded(goes(link, 4), lambda link=link: give_tile(link, 1).start())
    spread(2, gathered(1))
    send_step(2, False)

    def line_of(link, s):
        if link == 0:
            return 2 + jnp.where(late_pair, 1, 0), s - 2 * jnp.where(late_pair, 1, 0)
        if link == 1:
            return (4, s) if s < 4 else (5, s - 4 + 2 * is_m)
        return (6, (s + 2 * is_m) % 4) if s < 4 else (7, s - 2)

    def set_ranks(unit, tile, at):
        both = [tiles[tile, pl.ds(4 * j + at, 1), :] for j in range(2)]
        cranks[unit] = jnp.concatenate(both, axis=1)
        own = tiles[tile, pl.ds(4 * core + at, 1), :]
        rranks[unit] = jnp.broadcast_to(own, (UNIT, UNIT)).T

    for i in range(PER):
        set_ranks(i, 0, i)
    for link in range(3):
        guarded(comes(link, 4), lambda link=link: take_tile(link, 1).wait_recv())
        for s in range(STEPS):
            guarded(held(link, s), lambda link=link, s=s: set_ranks(bases[link] + s, *line_of(link, s)))

    whole = gathered(2)
    send_step(3, False)
    mean = whole[0:8] / whole[8:9]
    center[...] = jnp.concatenate([mean[i : i + 1] for i in range(8)], axis=1)

    half = pl.ds(pl.multiple_of(core * UNIT, UNIT), UNIT)
    theirs = pl.ds(pl.multiple_of((1 - core) * UNIT, UNIT), UNIT)

    def normalise(unit):
        shifted = raw[unit].astype(jnp.float32) - center[...]
        scale = lax.rsqrt(jnp.sum(shifted * shifted, axis=-1, keepdims=True) + 1e-06)
        norm[unit, half, :] = (shifted * scale).astype(jnp.bfloat16)

    def exchange(unit, rows):
        return pltpu.make_async_remote_copy(
            src_ref=norm.at[unit, rows], dst_ref=norm.at[unit, rows], send_sem=core_send.at[unit], recv_sem=core_recv.at[unit],
            device_id=sibling, device_id_type=MESH,
        )

    def prepare(unit):
        normalise(unit)
        exchange(unit, half).start()

    def pair(u, v):
        rows = norm[pl.ds(u, 2), half, :].reshape(2 * UNIT, 1024)
        cosines = lax.dot_general(rows, norm[v], (((1,), (1,)), ((), ())), preferred_element_type=jnp.float32)
        own = rranks[pl.ds(u, 2)].reshape(2 * UNIT, UNIT)
        best_rows = rowacc[pl.ds(u, 2)].reshape(2 * UNIT, UNIT)
        for h in range(2):
            at = slice(UNIT * h, UNIT * (h + 1))
            part, other = cosines[:, at], cranks[v, :, at]
            best_rows = jnp.maximum(best_rows, jnp.where(other < own, part, -1.0))
            up = jnp.where(own < other, part, -1.0)
            colacc[v, :, at] = jnp.maximum(colacc[v, :, at], jnp.max(up.reshape(2 * UNIT // 8, 8, UNIT), axis=0))
        rowacc[pl.ds(u, 2)] = best_rows.reshape(2, UNIT, UNIT)

    plans = [jobs_of(r) for r in range(3)]

    def run_jobs(part):
        lists = [plan[part] + plan[part][-1:] * (-len(plan[part]) % WIDE) for plan in plans]
        lists.append(lists[2])
        longest = max(len(jobs) for jobs in lists)
        if not longest:
            return
        codes = []
        for j in range(longest):
            at = [jobs[j][0] * 32 + jobs[j][1] if j < len(jobs) else 0 for jobs in lists]
            codes.append(pick(role, at))

        def body(j, _):
            for k in range(WIDE):
                code = codes[k]
                for i in range(1, longest // WIDE):
                    code = jnp.where(j == i, codes[WIDE * i + k], code)
                pair(code // 32, code % 32)
            return 0

        lax.fori_loop(0, pick(role, [len(jobs) // WIDE for jobs in lists]), body, 0)

    def own_unit(unit, _):
        prepare(unit)
        return 0

    lax.fori_loop(0, PER, own_unit, 0)

    def prepare_step(s):
        arrive(s)
        for link in range(3):
            guarded(held(link, s), lambda link=link: prepare(bases[link] + s))

    def exchanged(s):
        for link in range(3):
            guarded(held(link, s), lambda link=link: exchange(bases[link] + s, theirs).wait_recv())

    for s in range(AHEAD):
        prepare_step(s)
    for i in range(PER):
        exchange(i, theirs).wait_recv()
    run_jobs(0)
    for s in range(AHEAD):
        exchanged(s)
        run_jobs(1 + s)
    for s in range(AHEAD, STEPS):
        prepare_step(s)
        run_jobs(1 + AHEAD + 2 * (s - AHEAD))
        exchanged(s)
        run_jobs(2 + AHEAD + 2 * (s - AHEAD))

    def finish(unit, slot, at):
        best = jnp.max(colacc[unit], axis=0, keepdims=True)
        across_lanes = jnp.max(rowacc[unit].T, axis=0, keepdims=True)
        for j in range(2):
            part = best[:, UNIT * j : UNIT * (j + 1)]
            ret[slot, j, pl.ds(at, 1), :] = jnp.where(core == j, jnp.maximum(part, across_lanes), part)

    for link in range(3):
        for s in range(STEPS):
            slot = 1 + link if s < 4 or link == 0 else 4
            guarded(held(link, s), lambda link=link, s=s, slot=slot: finish(bases[link] + s, slot, line_of(link, s)[1]))
    owners = [
        actual(pick(role, (1, 0, 5, 2))),
        actual(pick(role, (3, 2, 3, 4))),
        actual(pick(role, (4, 5, 6, 6))),
        actual(pick(role, (7, 6, 7, 7))),
    ]

    def give(slot, j):
        return pltpu.make_async_remote_copy(
            src_ref=ret.at[slot, j], dst_ref=back.at[2 * chip + core], send_sem=ret_send.at[slot, j], recv_sem=ret_recv.at[2 * chip + core],
            device_id={"member": 2 * owners[slot - 1] + j}, device_id_type=MESH,
        )

    for slot in range(1, 5):
        for j in range(2):
            give(slot, j).start()
    for i in range(PER):
        finish(i, 0, i)
    to_sibling = pltpu.make_async_remote_copy(
        src_ref=ret.at[0, 1 - core], dst_ref=back.at[member], send_sem=ret_send.at[0, 0], recv_sem=ret_recv.at[member],
        device_id=sibling, device_id_type=MESH,
    )
    to_sibling.start()

    other_of = lambda c: (c % 4 + 2) % 4 + 4 * (1 - c // 4)
    givers = [
        actual(pick(role, (1, 0, 1, 1))),
        jnp.where(late_pair, actual(pick(role, (5, 5, 5, 2))), other_of(actual(pick(role, (1, 0, 0, 0))))),
        other_of(actual(pick(role, (2, 2, 0, 0)))),
        other_of(actual(pick(role, (5, 5, 5, 2)))),
    ]

    def take(source):
        return pltpu.make_async_remote_copy(
            src_ref=back.at[source], dst_ref=back.at[source], send_sem=ret_send.at[0, 1], recv_sem=ret_recv.at[source],
            device_id=sibling, device_id_type=MESH,
        )

    take(2 * chip + 1 - core).wait_recv()
    for giver in givers:
        for j in range(2):
            take(2 * giver + j).wait_recv()
    computes = lambda c: (c // 4) if c != 3 and c != 5 else 1 - c // 4
    for c in range(2):
        best = jnp.maximum(jnp.full((8, UNIT), -1.0, jnp.float32), jnp.where(mine == c, ret[0, core], -1.0))
        for source in range(16):
            if computes(source // 2) == c:
                best = jnp.maximum(best, back[source])
        for i in range(PER):
            out[c : c + 1, i * UNIT : (i + 1) * UNIT] = jnp.where(own_live[c * PER + i], best[i : i + 1], -1.0)

    with_sibling(core).wait_send()
    for link in range(3):
        give_tile(link, 0).wait_send()
        guarded(goes(link, 4), lambda link=link: give_tile(link, 1).wait_send())

    for axis in range(3):
        for i in range(1, 4):
            part(axis, i, False).wait_send()
    for s in range(STEPS):
        for link in range(3):
            guarded(goes(link, s), lambda link=link: outgoing(link, s).wait_send())
    for i in range(PER):
        exchange(i, half).wait_send()
    for s in range(STEPS):
        for link in range(3):
            guarded(held(link, s), lambda link=link: exchange(bases[link] + s, half).wait_send())
    for slot in range(1, 5):
        for j in range(2):
            give(slot, j).wait_send()
    to_sibling.wait_send()


def solution(mesh):
    units = LR + STEPS

    def local(embeddings, order_rank, lengths):
        d = embeddings.shape[-1]
        f32, dma = jnp.float32, pltpu.SemaphoreType.DMA
        return pl.pallas_call(
            kernel,
            out_shape=jax.ShapeDtypeStruct(order_rank.shape, f32),
            in_specs=[
                pl.BlockSpec(memory_space=pl.ANY),
                pl.BlockSpec(memory_space=pl.ANY),
                pl.BlockSpec(memory_space=pl.ANY),
            ],
            out_specs=pl.BlockSpec(memory_space=pltpu.VMEM),
            scratch_shapes=[
                pltpu.SMEM(lengths.shape, jnp.int32),
                pltpu.VMEM(order_rank.shape, jnp.int32),
                pltpu.VMEM((OTHER + PER, UNIT, d), jnp.bfloat16),
                pltpu.VMEM((units, 2 * UNIT, d), jnp.bfloat16),
                pltpu.VMEM((units, 1, 2 * UNIT), f32),
                pltpu.VMEM((units, UNIT, UNIT), f32),
                pltpu.VMEM((units, UNIT, UNIT), f32),
                pltpu.VMEM((units, 8, 2 * UNIT), f32),
                pltpu.VMEM((2, 24, UNIT), f32),
                pltpu.VMEM((3, 4, 16, UNIT), f32),
                pltpu.VMEM((8, 8, UNIT), f32),
                pltpu.VMEM((5, 2, 8, UNIT), f32),
                pltpu.VMEM((16, 8, UNIT), f32),
                pltpu.VMEM((1, d), f32),
                dma((4,)),
                dma((3, STEPS)),
                dma((3 * STEPS,)),
                dma((units,)),
                dma((units,)),
                dma((1,)),
                dma((1,)),
                dma((3, 4)),
                dma((3, 4)),
                dma((3, 2)),
                dma((8,)),
                dma((5, 2)),
                dma((16,)),
            ],
            compiler_params=pltpu.CompilerParams(collective_id=0, has_side_effects=True, vmem_limit_bytes=60 * 1024 * 1024),
            cost_estimate=pl.CostEstimate(flops=10_000_000_000, bytes_accessed=4_000_000, transcendentals=10_000),
        )(lengths, embeddings.reshape(2, PER, UNIT, d), order_rank)

    placed = (P("group", "member", None), P("group", "member"), P("group"))
    return jax.shard_map(local, mesh=mesh, in_specs=placed, out_specs=P("group", "member"), check_vma=False)
```

```python
import jax
import jax.numpy as jnp
from jax import lax
from jax.experimental import pallas as pl
from jax.experimental.pallas import tpu as pltpu
from jax.sharding import PartitionSpec as P

MESH = pl.DeviceIdType.MESH
UNIT = 128
PER = 4
STEPS = 6
LP, LQ, LR = 4, 10, 16
OTHER = 22
NO_RANK = 1e9
AHEAD = 2
LEAVE, LAST_LEAVE = 4, 4
WIDE, LAST_WIDE = 4, 7
NONE = -1


def needed(role):
    own, q, r = (0, 2), (LQ, LQ + 2, LQ + 4), (LR, LR + 2, LR + 4)
    p = (LP + 2, LP + 4) if role == 2 else (LP, LP + 2)
    columns = lambda firsts: [u + i for u in firsts for i in range(2)]
    jobs = []
    if role == 2:
        jobs += [(u, v) for u in own + r[:2] for v in columns(q)]
        jobs += [(u, v) for u in p for v in columns(q[2:])] + [(u, v) for u in q[:2] for v in columns(p)]
        jobs += [(u, v) for u in q for v in columns(q) if v >= u]
        jobs += [(u, v) for u in own for v in columns(own) if v >= u]
        jobs += [(u, v) for u in own for v in columns(r[:2])]
        jobs += [(r[0], v) for v in columns(r[:2])]
    else:
        jobs += [(u, v) for u in own + p for v in columns(q + r)]
        if role == 0:
            for a in range(3):
                for b in range(3):
                    jobs += [(q[a], v) for v in columns([r[b]])] if b >= a else [(r[b], v) for v in columns([q[a]])]
        else:
            jobs += [(u, v) for u in own + p for v in columns(own + p) if v >= u]
            jobs += [(u, v) for u in q[:2] for v in columns(r[:2])]
    return jobs


def jobs_of(role):
    def there(unit):
        return 0 if unit < LP else (unit - LP) % STEPS + 1

    ready = lambda job: max(there(job[0] + 1), there(job[1]))
    todo = sorted(needed(role), key=ready)
    plan, at = [], 0

    def take(limit, leave):
        nonlocal at
        able = sum(ready(job) <= limit for job in todo)
        until = max(at, able - leave)
        plan.append(todo[at:until])
        at = until

    take(0, 0)
    for s in range(AHEAD):
        take(s + 1, LEAVE if s == AHEAD - 1 else 0)
    for s in range(AHEAD, STEPS):
        take(s, 0)
        take(s + 1, 0 if s == STEPS - 1 else LAST_LEAVE if s == STEPS - 2 else LEAVE)
    return plan


def pick(index, values):
    out = jnp.int32(values[0])
    for i in range(1, len(values)):
        out = jnp.where(index == i, values[i], out)
    return out


def kernel(
    lengths_hbm, emb, order_hbm, out, lengths, order, raw, norm, cranks, rranks, rowacc, colacc, sums, parts, tiles, ret, back, center,
    load_sem, raw_send, raw_recv, core_send, core_recv, sum_send, sum_recv, part_send, part_recv, tile_send, tile_recv, ret_send, ret_recv,
):
    group, member = lax.axis_index("group"), lax.axis_index("member")
    core, x, y = member % 2, (member // 2) % 4, member // 8
    role = (x + 2 * y) % 4
    is_m = jnp.where(role == 3, 1, 0)
    mine = y + is_m * (1 - 2 * y)
    chip = 4 * y + x
    sibling = {"member": 2 * chip + 1 - core}

    def actual(c):
        cx, cy = c % 4, c // 4
        return (cx + 2 * mine) % 4 + 4 * (cy + mine * (1 - 2 * cy))

    xp, xm, yy = 4 * y + (x + 1) % 4, 4 * y + (x + 3) % 4, 4 * (1 - y) + x
    neighbour = [
        jnp.where(role == 0, xp, jnp.where(role == 3, yy, xm)),
        jnp.where((role == 1) | (role == 2), xp, xm),
        jnp.where(role == 3, xp, yy),
    ]
    bases = (LP, LQ, LR)
    landing = [
        pick(role, (LP, LP, LQ, LR)),
        pick(role, (LR, LP, LQ, LQ)),
        pick(role, (LR, LP, LR, LQ)),
    ]
    late_pair = role >= 2
    is_c = role == 1

    small = [
        pltpu.make_async_copy(lengths_hbm, lengths, load_sem.at[2]),
        pltpu.make_async_copy(order_hbm, order, load_sem.at[3]),
    ]
    for cp in small:
        cp.start()
    loads = []
    for i, (cluster, first) in enumerate(((mine, 0), (1 - mine, OTHER))):
        loads.append(pltpu.make_async_copy(emb.at[cluster], raw.at[pl.ds(first, PER)], load_sem.at[i]))
        loads[-1].start()
    barrier = pltpu.get_barrier_semaphore()
    z, wide_y = group % 4, 2 * (group // 4) + y

    def along(axis, i):
        if axis == 0:
            return {"group": 4 * (group // 4) + (z + i) % 4, "member": member}
        if axis == 1:
            to = (wide_y + i) % 4
            return {"group": 4 * (to // 2) + z, "member": 8 * (to % 2) + 2 * x + core}
        return {"group": group, "member": 8 * y + 2 * ((x + i) % 4) + core}

    for axis in range(3):
        for i in range(1, 4):
            pl.semaphore_signal(barrier, inc=1, device_id=along(axis, i), device_id_type=MESH)
    pl.semaphore_signal(barrier, inc=1, device_id=sibling, device_id_type=MESH)

    ret[...] = jnp.full(ret.shape, -1.0, jnp.float32)
    back[...] = jnp.full(back.shape, -1.0, jnp.float32)

    for cp in small:
        cp.wait()
    first_slot = member * (PER * UNIT)
    lane = lax.broadcasted_iota(jnp.int32, (1, UNIT), 1)
    own_ranks, own_live = [], []
    for c in range(2):
        for i in range(PER):
            is_live = first_slot + i * UNIT + lane < lengths[c]
            own_live.append(is_live)
            own = order[c : c + 1, i * UNIT : (i + 1) * UNIT].astype(jnp.float32)
            own_ranks.append(jnp.where(is_live, own, NO_RANK))
    by_cluster = [jnp.concatenate(own_ranks[PER * c : PER * (c + 1)], axis=0) for c in range(2)]
    first = mine == 0
    sums[core, 16:24, :] = jnp.concatenate(
        [jnp.where(first, by_cluster[0], by_cluster[1]), jnp.where(first, by_cluster[1], by_cluster[0])], axis=0
    )

    for cp in loads:
        cp.wait()
    row = lax.broadcasted_iota(jnp.int32, (UNIT, 1), 0)

    def add_unit(i, carry):
        total, count = carry
        other = i // PER
        cluster = mine + other * (1 - 2 * mine)
        at = i % PER
        is_live = first_slot + at * UNIT + row < lengths[cluster]
        values = jnp.where(is_live, raw[at + other * OTHER].astype(jnp.float32), 0.0)
        total = total + jnp.sum(values.reshape(UNIT // 8, 8, -1), axis=0)
        count = count + jnp.sum(is_live.astype(jnp.float32), axis=0, keepdims=True)
        return total, count

    total, count = lax.fori_loop(0, 2 * PER, add_unit, (jnp.zeros((8, 1024), jnp.float32), jnp.zeros((1, 1), jnp.float32)))
    total = jnp.sum(total, axis=0, keepdims=True)
    rows_out = [total[:, 128 * i : 128 * (i + 1)] for i in range(8)]
    rows_out += [jnp.broadcast_to(count, (1, 128))] + [jnp.zeros((7, 128), jnp.float32)]
    sums[core, 0:16, :] = jnp.concatenate(rows_out, axis=0)

    pl.semaphore_wait(barrier, 10)

    def with_sibling(slot):
        return pltpu.make_async_remote_copy(
            src_ref=sums.at[slot], dst_ref=sums.at[slot], send_sem=sum_send.at[0], recv_sem=sum_recv.at[0],
            device_id=sibling, device_id_type=MESH,
        )

    with_sibling(core).start()

    def source_of(link, s):
        if link == 0:
            return s if s < 4 else LR + s - 4
        by_c = (OTHER + (2 if link == 1 else 0) + s) if s < 2 else ((LR if link == 1 else LQ) + s - 2)
        by_h = OTHER + ((s + 2) % 4 if link == 1 else s % 4)
        by_lm = OTHER + s if s < 4 else LP + s - 4
        return pick(role, (by_h, by_c, by_lm, by_lm))

    def goes(link, s):
        if s < 4:
            return None
        return late_pair if link == 0 else role != 0

    def outgoing(link, s):
        return pltpu.make_async_remote_copy(
            src_ref=raw.at[source_of(link, s)], dst_ref=raw.at[landing[link] + s],
            send_sem=raw_send.at[link, s], recv_sem=raw_recv.at[landing[link] - LP + s],
            device_id={"member": 2 * neighbour[link] + core}, device_id_type=MESH,
        )

    def arriving(link, s):
        unit = bases[link] + s
        return pltpu.make_async_remote_copy(
            src_ref=raw.at[unit], dst_ref=raw.at[unit], send_sem=raw_send.at[link, s], recv_sem=raw_recv.at[unit - LP],
            device_id={"member": 2 * neighbour[link] + core}, device_id_type=MESH,
        )

    def comes(link, s):
        if s < 4 or link == 1:
            return None
        return late_pair if link == 0 else jnp.logical_not(late_pair)

    def guarded(condition, do):
        if condition is None:
            do()
        else:
            pl.when(condition)(do)

    def held(link, s):
        if link == 0 and s < 2:
            return jnp.logical_not(late_pair)
        return comes(link, s)

    def send_step(s, everyone, links=(0, 1, 2)):
        for link in links:
            condition = None if everyone or link == 0 else jnp.logical_not(is_c)
            guarded(condition, lambda link=link: outgoing(link, s).start())

    def forward(s):
        if s in (2, 3):

            @pl.when(late_pair)
            def _():
                for link in range(3):
                    outgoing(link, s + 2).start()

    def arrive(s):
        for link in (2, 1, 0):
            guarded(comes(link, s), lambda link=link: arriving(link, s).wait_recv())
            if s < 4 and link:

                @pl.when(is_c)
                def _():
                    outgoing(3 - link, s + 2).start()

        forward(s)

    send_step(0, True)
    rowacc[...] = jnp.full(rowacc.shape, -1.0, jnp.float32)
    colacc[...] = jnp.full(colacc.shape, -1.0, jnp.float32)

    with_sibling(1 - core).wait_recv()
    place = (z, wide_y, x)

    def part(axis, i, source):
        at = (place[axis] + 4 - i) % 4 if source else place[axis]
        return pltpu.make_async_remote_copy(
            src_ref=parts.at[axis, at], dst_ref=parts.at[axis, at], send_sem=part_send.at[axis, i], recv_sem=part_recv.at[axis, at],
            device_id=along(axis, i), device_id_type=MESH,
        )

    def spread(axis, value):
        parts[axis, place[axis]] = value
        for i in range(1, 4):
            part(axis, i, False).start()

    def gathered(axis):
        for i in range(1, 4):
            part(axis, i, True).wait_recv()
        return (parts[axis, 0] + parts[axis, 1]) + (parts[axis, 2] + parts[axis, 3])

    spread(0, sums[0, 0:16, :] + sums[1, 0:16, :])

    for i in range(2):
        lines = slice(16 + 4 * i, 20 + 4 * i)
        tiles[i] = jnp.concatenate([sums[0, lines, :], sums[1, lines, :]], axis=0)
    far_link = [pick(role, (0, 0, 1, 2)), pick(role, (2, 0, 1, 1)), pick(role, (2, 0, 2, 1))]

    def give_tile(link, again):
        if not again:
            source = 0 if link == 0 else 1
        elif link == 0:
            source = 6
        else:
            source = jnp.where(is_c, 6 if link == 1 else 4, 2)
        landed = 2 + 2 * far_link[link] + again
        return pltpu.make_async_remote_copy(
            src_ref=tiles.at[source], dst_ref=tiles.at[landed], send_sem=tile_send.at[link, again], recv_sem=tile_recv.at[landed],
            device_id={"member": 2 * neighbour[link] + core}, device_id_type=MESH,
        )

    def take_tile(link, again):
        at = 2 + 2 * link + again
        return pltpu.make_async_remote_copy(
            src_ref=tiles.at[at], dst_ref=tiles.at[at], send_sem=tile_send.at[link, again], recv_sem=tile_recv.at[at],
            device_id={"member": 2 * neighbour[link] + core}, device_id_type=MESH,
        )

    for link in range(3):
        give_tile(link, 0).start()

    spread(1, gathered(0))
    send_step(1, True)
    for link in range(3):
        take_tile(link, 0).wait_recv()
    for link in range(3):
        guarded(goes(link, 4), lambda link=link: give_tile(link, 1).start())
    spread(2, gathered(1))
    send_step(2, False)

    def line_of(link, s):
        if link == 0:
            return 2 + jnp.where(late_pair, 1, 0), s - 2 * jnp.where(late_pair, 1, 0)
        if link == 1:
            return (4, s) if s < 4 else (5, s - 4 + 2 * is_m)
        return (6, (s + 2 * is_m) % 4) if s < 4 else (7, s - 2)

    def set_ranks(unit, tile, at):
        both = [tiles[tile, pl.ds(4 * j + at, 1), :] for j in range(2)]
        cranks[unit] = jnp.concatenate(both, axis=1)
        own = tiles[tile, pl.ds(4 * core + at, 1), :]
        rranks[unit] = jnp.broadcast_to(own, (UNIT, UNIT)).T

    for i in range(PER):
        set_ranks(i, 0, i)
    for link in range(3):
        guarded(comes(link, 4), lambda link=link: take_tile(link, 1).wait_recv())
        for s in range(STEPS):
            guarded(held(link, s), lambda link=link, s=s: set_ranks(bases[link] + s, *line_of(link, s)))

    send_step(3, False, (1, 2))
    arrive(0)
    whole = gathered(2)
    send_step(3, False, (0,))
    mean = whole[0:8] / whole[8:9]
    center[...] = jnp.concatenate([mean[i : i + 1] for i in range(8)], axis=1)

    half = pl.ds(pl.multiple_of(core * UNIT, UNIT), UNIT)
    theirs = pl.ds(pl.multiple_of((1 - core) * UNIT, UNIT), UNIT)

    def normalise(unit):
        shifted = raw[unit].astype(jnp.float32) - center[...]
        scale = lax.rsqrt(jnp.sum(shifted * shifted, axis=-1, keepdims=True) + 1e-06)
        norm[unit, half, :] = (shifted * scale).astype(jnp.bfloat16)

    def exchange(unit, rows):
        return pltpu.make_async_remote_copy(
            src_ref=norm.at[unit, rows], dst_ref=norm.at[unit, rows], send_sem=core_send.at[unit], recv_sem=core_recv.at[unit],
            device_id=sibling, device_id_type=MESH,
        )

    def prepare(unit):
        normalise(unit)
        exchange(unit, half).start()

    def pair(u, v):
        rows = norm[pl.ds(u, 2), half, :].reshape(2 * UNIT, 1024)
        cosines = lax.dot_general(rows, norm[v], (((1,), (1,)), ((), ())), preferred_element_type=jnp.float32)
        own = rranks[pl.ds(u, 2)].reshape(2 * UNIT, UNIT)
        best_rows = rowacc[pl.ds(u, 2)].reshape(2 * UNIT, UNIT)
        for h in range(2):
            at = slice(UNIT * h, UNIT * (h + 1))
            part, other = cosines[:, at], cranks[v, :, at]
            best_rows = jnp.maximum(best_rows, jnp.where(other < own, part, -1.0))
            up = jnp.where(own < other, part, -1.0)
            colacc[v, :, at] = jnp.maximum(colacc[v, :, at], jnp.max(up.reshape(2 * UNIT // 8, 8, UNIT), axis=0))
        rowacc[pl.ds(u, 2)] = best_rows.reshape(2, UNIT, UNIT)

    plans = [jobs_of(r) for r in range(3)]

    def run_jobs(part, wide=WIDE):
        lists = [plan[part] + plan[part][-1:] * (-len(plan[part]) % wide) for plan in plans]
        lists.append(lists[2])
        longest = max(len(jobs) for jobs in lists)
        if not longest:
            return
        codes = []
        for j in range(longest):
            at = [jobs[j][0] * 32 + jobs[j][1] if j < len(jobs) else 0 for jobs in lists]
            codes.append(pick(role, at))

        def body(j, _):
            for k in range(wide):
                code = codes[k]
                for i in range(1, longest // wide):
                    code = jnp.where(j == i, codes[wide * i + k], code)
                pair(code // 32, code % 32)
            return 0

        lax.fori_loop(0, pick(role, [len(jobs) // wide for jobs in lists]), body, 0)

    def own_unit(unit, _):
        prepare(unit)
        return 0

    arrive(1)
    lax.fori_loop(0, PER, own_unit, 0)

    def prepare_step(s):
        if s > 1:
            arrive(s)
        for link in range(3):
            guarded(held(link, s), lambda link=link: prepare(bases[link] + s))

    def exchanged(s):
        for link in range(3):
            guarded(held(link, s), lambda link=link: exchange(bases[link] + s, theirs).wait_recv())

    for s in range(AHEAD):
        prepare_step(s)
    for i in range(PER):
        exchange(i, theirs).wait_recv()
    run_jobs(0)
    for s in range(AHEAD):
        exchanged(s)
        run_jobs(1 + s)
    for s in range(AHEAD, STEPS):
        prepare_step(s)
        run_jobs(1 + AHEAD + 2 * (s - AHEAD))
        exchanged(s)
        run_jobs(2 + AHEAD + 2 * (s - AHEAD), LAST_WIDE if s == STEPS - 1 else WIDE)

    def finish(unit, slot, at):
        best = jnp.max(colacc[unit], axis=0, keepdims=True)
        across_lanes = jnp.max(rowacc[unit].T, axis=0, keepdims=True)
        for j in range(2):
            part = best[:, UNIT * j : UNIT * (j + 1)]
            ret[slot, j, pl.ds(at, 1), :] = jnp.where(core == j, jnp.maximum(part, across_lanes), part)

    owners = [
        actual(pick(role, (1, 0, 5, 2))),
        actual(pick(role, (3, 2, 3, 4))),
        actual(pick(role, (4, 5, 6, 6))),
        actual(pick(role, (7, 6, 7, 7))),
    ]

    def give(slot, j):
        return pltpu.make_async_remote_copy(
            src_ref=ret.at[slot, j], dst_ref=back.at[2 * chip + core], send_sem=ret_send.at[slot, j], recv_sem=ret_recv.at[2 * chip + core],
            device_id={"member": 2 * owners[slot - 1] + j}, device_id_type=MESH,
        )

    slots = [[(link, s) for s in range(STEPS) if s < 4 or link == 0] for link in range(3)]
    slots.append([(link, s) for link in (1, 2) for s in (4, 5)])
    for slot in (4, 1, 2, 3):
        for link, s in slots[slot - 1]:
            guarded(held(link, s), lambda link=link, s=s, slot=slot: finish(bases[link] + s, slot, line_of(link, s)[1]))
        for j in range(2):
            give(slot, j).start()
    for i in range(PER):
        finish(i, 0, i)
    to_sibling = pltpu.make_async_remote_copy(
        src_ref=ret.at[0, 1 - core], dst_ref=back.at[member], send_sem=ret_send.at[0, 0], recv_sem=ret_recv.at[member],
        device_id=sibling, device_id_type=MESH,
    )
    to_sibling.start()

    other_of = lambda c: (c % 4 + 2) % 4 + 4 * (1 - c // 4)
    givers = [
        actual(pick(role, (1, 0, 1, 1))),
        jnp.where(late_pair, actual(pick(role, (5, 5, 5, 2))), other_of(actual(pick(role, (1, 0, 0, 0))))),
        other_of(actual(pick(role, (2, 2, 0, 0)))),
        other_of(actual(pick(role, (5, 5, 5, 2)))),
    ]

    def take(source):
        return pltpu.make_async_remote_copy(
            src_ref=back.at[source], dst_ref=back.at[source], send_sem=ret_send.at[0, 1], recv_sem=ret_recv.at[source],
            device_id=sibling, device_id_type=MESH,
        )

    take(2 * chip + 1 - core).wait_recv()
    for giver in givers:
        for j in range(2):
            take(2 * giver + j).wait_recv()
    computes = lambda c: (c // 4) if c != 3 and c != 5 else 1 - c // 4
    for c in range(2):
        best = jnp.maximum(jnp.full((8, UNIT), -1.0, jnp.float32), jnp.where(mine == c, ret[0, core], -1.0))
        for source in range(16):
            if computes(source // 2) == c:
                best = jnp.maximum(best, back[source])
        for i in range(PER):
            out[c : c + 1, i * UNIT : (i + 1) * UNIT] = jnp.where(own_live[c * PER + i], best[i : i + 1], -1.0)

    with_sibling(core).wait_send()
    for link in range(3):
        give_tile(link, 0).wait_send()
        guarded(goes(link, 4), lambda link=link: give_tile(link, 1).wait_send())

    for axis in range(3):
        for i in range(1, 4):
            part(axis, i, False).wait_send()
    for s in range(STEPS):
        for link in range(3):
            guarded(goes(link, s), lambda link=link: outgoing(link, s).wait_send())
    for i in range(PER):
        exchange(i, half).wait_send()
    for s in range(STEPS):
        for link in range(3):
            guarded(held(link, s), lambda link=link: exchange(bases[link] + s, half).wait_send())
    for slot in range(1, 5):
        for j in range(2):
            give(slot, j).wait_send()
    to_sibling.wait_send()


def solution(mesh):
    units = LR + STEPS

    def local(embeddings, order_rank, lengths):
        d = embeddings.shape[-1]
        f32, dma = jnp.float32, pltpu.SemaphoreType.DMA
        return pl.pallas_call(
            kernel,
            out_shape=jax.ShapeDtypeStruct(order_rank.shape, f32),
            in_specs=[
                pl.BlockSpec(memory_space=pl.ANY),
                pl.BlockSpec(memory_space=pl.ANY),
                pl.BlockSpec(memory_space=pl.ANY),
            ],
            out_specs=pl.BlockSpec(memory_space=pltpu.VMEM),
            scratch_shapes=[
                pltpu.SMEM(lengths.shape, jnp.int32),
                pltpu.VMEM(order_rank.shape, jnp.int32),
                pltpu.VMEM((OTHER + PER, UNIT, d), jnp.bfloat16),
                pltpu.VMEM((units, 2 * UNIT, d), jnp.bfloat16),
                pltpu.VMEM((units, 1, 2 * UNIT), f32),
                pltpu.VMEM((units, UNIT, UNIT), f32),
                pltpu.VMEM((units, UNIT, UNIT), f32),
                pltpu.VMEM((units, 8, 2 * UNIT), f32),
                pltpu.VMEM((2, 24, UNIT), f32),
                pltpu.VMEM((3, 4, 16, UNIT), f32),
                pltpu.VMEM((8, 8, UNIT), f32),
                pltpu.VMEM((5, 2, 8, UNIT), f32),
                pltpu.VMEM((16, 8, UNIT), f32),
                pltpu.VMEM((1, d), f32),
                dma((4,)),
                dma((3, STEPS)),
                dma((3 * STEPS,)),
                dma((units,)),
                dma((units,)),
                dma((1,)),
                dma((1,)),
                dma((3, 4)),
                dma((3, 4)),
                dma((3, 2)),
                dma((8,)),
                dma((5, 2)),
                dma((16,)),
            ],
            compiler_params=pltpu.CompilerParams(collective_id=0, has_side_effects=True, vmem_limit_bytes=60 * 1024 * 1024),
            cost_estimate=pl.CostEstimate(flops=10_000_000_000, bytes_accessed=4_000_000, transcendentals=10_000),
        )(lengths, embeddings.reshape(2, PER, UNIT, d), order_rank)

    placed = (P("group", "member", None), P("group", "member"), P("group"))
    return jax.shard_map(local, mesh=mesh, in_specs=placed, out_specs=P("group", "member"), check_vma=False)
```

```python
import jax
import jax.numpy as jnp
from jax import lax
from jax.experimental import pallas as pl
from jax.experimental.pallas import tpu as pltpu
from jax.sharding import PartitionSpec as P

MESH = pl.DeviceIdType.MESH
UNIT = 128
PER = 4
STEPS = 6
LP, LQ, LR = 4, 10, 16
OTHER = 22
NO_RANK = 1e9
AHEAD = 2
LEAVE, LAST_LEAVE = 4, 4
WIDE, LAST_WIDE = 4, 14
NONE = -1


def needed(role):
    own, q, r = (0, 2), (LQ, LQ + 2, LQ + 4), (LR, LR + 2, LR + 4)
    p = (LP + 2, LP + 4) if role == 2 else (LP, LP + 2)
    columns = lambda firsts: [u + i for u in firsts for i in range(2)]
    jobs = []
    if role == 2:
        jobs += [(u, v) for u in own + r[:2] for v in columns(q)]
        jobs += [(u, v) for u in p for v in columns(q[2:])] + [(u, v) for u in q[:2] for v in columns(p)]
        jobs += [(u, v) for u in q for v in columns(q) if v >= u]
        jobs += [(u, v) for u in own for v in columns(own) if v >= u]
        jobs += [(u, v) for u in own for v in columns(r[:2])]
        jobs += [(r[0], v) for v in columns(r[:2])]
    else:
        jobs += [(u, v) for u in own + p for v in columns(q + r)]
        if role == 0:
            for a in range(3):
                for b in range(3):
                    jobs += [(q[a], v) for v in columns([r[b]])] if b >= a else [(r[b], v) for v in columns([q[a]])]
        else:
            jobs += [(u, v) for u in own + p for v in columns(own + p) if v >= u]
            jobs += [(u, v) for u in q[:2] for v in columns(r[:2])]
    return jobs


def jobs_of(role):
    def there(unit):
        return 0 if unit < LP else (unit - LP) % STEPS + 1

    ready = lambda job: max(there(job[0] + 1), there(job[1]))
    todo = sorted(needed(role), key=ready)
    plan, at = [], 0

    def take(limit, leave):
        nonlocal at
        able = sum(ready(job) <= limit for job in todo)
        until = max(at, able - leave)
        plan.append(todo[at:until])
        at = until

    take(0, 0)
    for s in range(AHEAD):
        take(s + 1, LEAVE if s == AHEAD - 1 else 0)
    for s in range(AHEAD, STEPS):
        take(s, 0)
        take(s + 1, 0 if s == STEPS - 1 else LAST_LEAVE if s == STEPS - 2 else LEAVE)
    return plan


def pick(index, values):
    out = jnp.int32(values[0])
    for i in range(1, len(values)):
        out = jnp.where(index == i, values[i], out)
    return out


def kernel(
    lengths_hbm, emb, order_hbm, out, lengths, order, raw, norm, cranks, rranks, rowacc, colacc, sums, parts, tiles, ret, back, center,
    load_sem, raw_send, raw_recv, core_send, core_recv, sum_send, sum_recv, part_send, part_recv, tile_send, tile_recv, ret_send, ret_recv,
):
    group, member = lax.axis_index("group"), lax.axis_index("member")
    core, x, y = member % 2, (member // 2) % 4, member // 8
    role = (x + 2 * y) % 4
    is_m = jnp.where(role == 3, 1, 0)
    mine = y + is_m * (1 - 2 * y)
    chip = 4 * y + x
    sibling = {"member": 2 * chip + 1 - core}

    def actual(c):
        cx, cy = c % 4, c // 4
        return (cx + 2 * mine) % 4 + 4 * (cy + mine * (1 - 2 * cy))

    xp, xm, yy = 4 * y + (x + 1) % 4, 4 * y + (x + 3) % 4, 4 * (1 - y) + x
    neighbour = [
        jnp.where(role == 0, xp, jnp.where(role == 3, yy, xm)),
        jnp.where((role == 1) | (role == 2), xp, xm),
        jnp.where(role == 3, xp, yy),
    ]
    bases = (LP, LQ, LR)
    landing = [
        pick(role, (LP, LP, LQ, LR)),
        pick(role, (LR, LP, LQ, LQ)),
        pick(role, (LR, LP, LR, LQ)),
    ]
    late_pair = role >= 2
    is_c = role == 1

    small = [
        pltpu.make_async_copy(lengths_hbm, lengths, load_sem.at[2]),
        pltpu.make_async_copy(order_hbm, order, load_sem.at[3]),
    ]
    for cp in small:
        cp.start()
    loads = []
    for i, (cluster, first) in enumerate(((mine, 0), (1 - mine, OTHER))):
        loads.append(pltpu.make_async_copy(emb.at[cluster], raw.at[pl.ds(first, PER)], load_sem.at[i]))
        loads[-1].start()
    barrier = pltpu.get_barrier_semaphore()
    z, wide_y = group % 4, 2 * (group // 4) + y

    def along(axis, i):
        if axis == 0:
            return {"group": 4 * (group // 4) + (z + i) % 4, "member": member}
        if axis == 1:
            to = (wide_y + i) % 4
            return {"group": 4 * (to // 2) + z, "member": 8 * (to % 2) + 2 * x + core}
        return {"group": group, "member": 8 * y + 2 * ((x + i) % 4) + core}

    for axis in range(3):
        for i in range(1, 4):
            pl.semaphore_signal(barrier, inc=1, device_id=along(axis, i), device_id_type=MESH)
    pl.semaphore_signal(barrier, inc=1, device_id=sibling, device_id_type=MESH)

    ret[...] = jnp.full(ret.shape, -1.0, jnp.float32)
    back[...] = jnp.full(back.shape, -1.0, jnp.float32)

    for cp in small:
        cp.wait()
    first_slot = member * (PER * UNIT)
    lane = lax.broadcasted_iota(jnp.int32, (1, UNIT), 1)
    own_ranks, own_live = [], []
    for c in range(2):
        for i in range(PER):
            is_live = first_slot + i * UNIT + lane < lengths[c]
            own_live.append(is_live)
            own = order[c : c + 1, i * UNIT : (i + 1) * UNIT].astype(jnp.float32)
            own_ranks.append(jnp.where(is_live, own, NO_RANK))
    by_cluster = [jnp.concatenate(own_ranks[PER * c : PER * (c + 1)], axis=0) for c in range(2)]
    first = mine == 0
    sums[core, 16:24, :] = jnp.concatenate(
        [jnp.where(first, by_cluster[0], by_cluster[1]), jnp.where(first, by_cluster[1], by_cluster[0])], axis=0
    )

    for cp in loads:
        cp.wait()
    row = lax.broadcasted_iota(jnp.int32, (UNIT, 1), 0)

    def add_unit(i, carry):
        total, count = carry
        other = i // PER
        cluster = mine + other * (1 - 2 * mine)
        at = i % PER
        is_live = first_slot + at * UNIT + row < lengths[cluster]
        values = jnp.where(is_live, raw[at + other * OTHER].astype(jnp.float32), 0.0)
        total = total + jnp.sum(values.reshape(UNIT // 8, 8, -1), axis=0)
        count = count + jnp.sum(is_live.astype(jnp.float32), axis=0, keepdims=True)
        return total, count

    total, count = lax.fori_loop(0, 2 * PER, add_unit, (jnp.zeros((8, 1024), jnp.float32), jnp.zeros((1, 1), jnp.float32)))
    total = jnp.sum(total, axis=0, keepdims=True)
    rows_out = [total[:, 128 * i : 128 * (i + 1)] for i in range(8)]
    rows_out += [jnp.broadcast_to(count, (1, 128))] + [jnp.zeros((7, 128), jnp.float32)]
    sums[core, 0:16, :] = jnp.concatenate(rows_out, axis=0)

    pl.semaphore_wait(barrier, 10)

    def with_sibling(slot):
        return pltpu.make_async_remote_copy(
            src_ref=sums.at[slot], dst_ref=sums.at[slot], send_sem=sum_send.at[0], recv_sem=sum_recv.at[0],
            device_id=sibling, device_id_type=MESH,
        )

    with_sibling(core).start()

    def source_of(link, s):
        if link == 0:
            return s if s < 4 else LR + s - 4
        by_c = (OTHER + (2 if link == 1 else 0) + s) if s < 2 else ((LR if link == 1 else LQ) + s - 2)
        by_h = OTHER + ((s + 2) % 4 if link == 1 else s % 4)
        by_lm = OTHER + s if s < 4 else LP + s - 4
        return pick(role, (by_h, by_c, by_lm, by_lm))

    def goes(link, s):
        if s < 4:
            return None
        return late_pair if link == 0 else role != 0

    def outgoing(link, s):
        return pltpu.make_async_remote_copy(
            src_ref=raw.at[source_of(link, s)], dst_ref=raw.at[landing[link] + s],
            send_sem=raw_send.at[link, s], recv_sem=raw_recv.at[landing[link] - LP + s],
            device_id={"member": 2 * neighbour[link] + core}, device_id_type=MESH,
        )

    def arriving(link, s):
        unit = bases[link] + s
        return pltpu.make_async_remote_copy(
            src_ref=raw.at[unit], dst_ref=raw.at[unit], send_sem=raw_send.at[link, s], recv_sem=raw_recv.at[unit - LP],
            device_id={"member": 2 * neighbour[link] + core}, device_id_type=MESH,
        )

    def comes(link, s):
        if s < 4 or link == 1:
            return None
        return late_pair if link == 0 else jnp.logical_not(late_pair)

    def guarded(condition, do):
        if condition is None:
            do()
        else:
            pl.when(condition)(do)

    def held(link, s):
        if link == 0 and s < 2:
            return jnp.logical_not(late_pair)
        return comes(link, s)

    def send_step(s, everyone, links=(0, 1, 2)):
        for link in links:
            condition = None if everyone or link == 0 else jnp.logical_not(is_c)
            guarded(condition, lambda link=link: outgoing(link, s).start())

    def forward(s):
        if s in (2, 3):

            @pl.when(late_pair)
            def _():
                for link in range(3):
                    outgoing(link, s + 2).start()

    def arrive(s):
        for link in (2, 1, 0):
            guarded(comes(link, s), lambda link=link: arriving(link, s).wait_recv())
            if s < 4 and link:

                @pl.when(is_c)
                def _():
                    outgoing(3 - link, s + 2).start()

        forward(s)

    send_step(0, True)
    rowacc[...] = jnp.full(rowacc.shape, -1.0, jnp.float32)
    colacc[...] = jnp.full(colacc.shape, -1.0, jnp.float32)

    with_sibling(1 - core).wait_recv()
    place = (z, wide_y, x)

    def part(axis, i, source):
        at = (place[axis] + 4 - i) % 4 if source else place[axis]
        return pltpu.make_async_remote_copy(
            src_ref=parts.at[axis, at], dst_ref=parts.at[axis, at], send_sem=part_send.at[axis, i], recv_sem=part_recv.at[axis, at],
            device_id=along(axis, i), device_id_type=MESH,
        )

    def spread(axis, value):
        parts[axis, place[axis]] = value
        for i in range(1, 4):
            part(axis, i, False).start()

    def gathered(axis):
        for i in range(1, 4):
            part(axis, i, True).wait_recv()
        return (parts[axis, 0] + parts[axis, 1]) + (parts[axis, 2] + parts[axis, 3])

    spread(0, sums[0, 0:16, :] + sums[1, 0:16, :])

    for i in range(2):
        lines = slice(16 + 4 * i, 20 + 4 * i)
        tiles[i] = jnp.concatenate([sums[0, lines, :], sums[1, lines, :]], axis=0)
    far_link = [pick(role, (0, 0, 1, 2)), pick(role, (2, 0, 1, 1)), pick(role, (2, 0, 2, 1))]

    def give_tile(link, again):
        if not again:
            source = 0 if link == 0 else 1
        elif link == 0:
            source = 6
        else:
            source = jnp.where(is_c, 6 if link == 1 else 4, 2)
        landed = 2 + 2 * far_link[link] + again
        return pltpu.make_async_remote_copy(
            src_ref=tiles.at[source], dst_ref=tiles.at[landed], send_sem=tile_send.at[link, again], recv_sem=tile_recv.at[landed],
            device_id={"member": 2 * neighbour[link] + core}, device_id_type=MESH,
        )

    def take_tile(link, again):
        at = 2 + 2 * link + again
        return pltpu.make_async_remote_copy(
            src_ref=tiles.at[at], dst_ref=tiles.at[at], send_sem=tile_send.at[link, again], recv_sem=tile_recv.at[at],
            device_id={"member": 2 * neighbour[link] + core}, device_id_type=MESH,
        )

    for link in range(3):
        give_tile(link, 0).start()

    spread(1, gathered(0))
    send_step(1, True)
    for link in range(3):
        take_tile(link, 0).wait_recv()
    for link in range(3):
        guarded(goes(link, 4), lambda link=link: give_tile(link, 1).start())
    spread(2, gathered(1))
    send_step(2, False)

    def line_of(link, s):
        if link == 0:
            return 2 + jnp.where(late_pair, 1, 0), s - 2 * jnp.where(late_pair, 1, 0)
        if link == 1:
            return (4, s) if s < 4 else (5, s - 4 + 2 * is_m)
        return (6, (s + 2 * is_m) % 4) if s < 4 else (7, s - 2)

    def set_ranks(unit, tile, at):
        both = [tiles[tile, pl.ds(4 * j + at, 1), :] for j in range(2)]
        cranks[unit] = jnp.concatenate(both, axis=1)
        own = tiles[tile, pl.ds(4 * core + at, 1), :]
        rranks[unit] = jnp.broadcast_to(own, (UNIT, UNIT)).T

    for i in range(PER):
        set_ranks(i, 0, i)
    for link in range(3):
        guarded(comes(link, 4), lambda link=link: take_tile(link, 1).wait_recv())
        for s in range(STEPS):
            guarded(held(link, s), lambda link=link, s=s: set_ranks(bases[link] + s, *line_of(link, s)))

    send_step(3, False, (1, 2))
    arrive(0)
    whole = gathered(2)
    send_step(3, False, (0,))
    mean = whole[0:8] / whole[8:9]
    center[...] = jnp.concatenate([mean[i : i + 1] for i in range(8)], axis=1)

    half = pl.ds(pl.multiple_of(core * UNIT, UNIT), UNIT)
    theirs = pl.ds(pl.multiple_of((1 - core) * UNIT, UNIT), UNIT)

    def normalise(unit):
        shifted = raw[unit].astype(jnp.float32) - center[...]
        scale = lax.rsqrt(jnp.sum(shifted * shifted, axis=-1, keepdims=True) + 1e-06)
        norm[unit, half, :] = (shifted * scale).astype(jnp.bfloat16)

    def exchange(unit, rows):
        return pltpu.make_async_remote_copy(
            src_ref=norm.at[unit, rows], dst_ref=norm.at[unit, rows], send_sem=core_send.at[unit], recv_sem=core_recv.at[unit],
            device_id=sibling, device_id_type=MESH,
        )

    def prepare(unit):
        normalise(unit)
        exchange(unit, half).start()

    def pair(u, v):
        rows = norm[pl.ds(u, 2), half, :].reshape(2 * UNIT, 1024)
        cosines = lax.dot_general(rows, norm[v], (((1,), (1,)), ((), ())), preferred_element_type=jnp.float32)
        own = rranks[pl.ds(u, 2)].reshape(2 * UNIT, UNIT)
        best_rows = rowacc[pl.ds(u, 2)].reshape(2 * UNIT, UNIT)
        for h in range(2):
            at = slice(UNIT * h, UNIT * (h + 1))
            part, other = cosines[:, at], cranks[v, :, at]
            best_rows = jnp.maximum(best_rows, jnp.where(other < own, part, -1.0))
            up = jnp.where(own < other, part, -1.0)
            colacc[v, :, at] = jnp.maximum(colacc[v, :, at], jnp.max(up.reshape(2 * UNIT // 8, 8, UNIT), axis=0))
        rowacc[pl.ds(u, 2)] = best_rows.reshape(2, UNIT, UNIT)

    plans = [jobs_of(r) for r in range(3)]

    def run_jobs(part, wide=WIDE):
        lists = [plan[part] + plan[part][-1:] * (-len(plan[part]) % wide) for plan in plans]
        lists.append(lists[2])
        longest = max(len(jobs) for jobs in lists)
        if not longest:
            return
        codes = []
        for j in range(longest):
            at = [jobs[j][0] * 32 + jobs[j][1] if j < len(jobs) else 0 for jobs in lists]
            codes.append(pick(role, at))

        def body(j, _):
            for k in range(wide):
                code = codes[k]
                for i in range(1, longest // wide):
                    code = jnp.where(j == i, codes[wide * i + k], code)
                pair(code // 32, code % 32)
            return 0

        lax.fori_loop(0, pick(role, [len(jobs) // wide for jobs in lists]), body, 0)

    def own_unit(unit, _):
        prepare(unit)
        return 0

    arrive(1)
    lax.fori_loop(0, PER, own_unit, 0)

    def prepare_step(s):
        if s > 1:
            arrive(s)
        for link in range(3):
            guarded(held(link, s), lambda link=link: prepare(bases[link] + s))

    def exchanged(s):
        for link in range(3):
            guarded(held(link, s), lambda link=link: exchange(bases[link] + s, theirs).wait_recv())

    for s in range(AHEAD):
        prepare_step(s)
    for i in range(PER):
        exchange(i, theirs).wait_recv()
    run_jobs(0)
    for s in range(AHEAD):
        exchanged(s)
        run_jobs(1 + s)
    for s in range(AHEAD, STEPS):
        prepare_step(s)
        run_jobs(1 + AHEAD + 2 * (s - AHEAD))
        exchanged(s)
        run_jobs(2 + AHEAD + 2 * (s - AHEAD), LAST_WIDE if s == STEPS - 1 else WIDE)

    def finish(unit, slot, at):
        best = jnp.max(colacc[unit], axis=0, keepdims=True)
        across_lanes = jnp.max(rowacc[unit].T, axis=0, keepdims=True)
        for j in range(2):
            part = best[:, UNIT * j : UNIT * (j + 1)]
            ret[slot, j, pl.ds(at, 1), :] = jnp.where(core == j, jnp.maximum(part, across_lanes), part)

    owners = [
        actual(pick(role, (1, 0, 5, 2))),
        actual(pick(role, (3, 2, 3, 4))),
        actual(pick(role, (4, 5, 6, 6))),
        actual(pick(role, (7, 6, 7, 7))),
    ]

    def give(slot, j):
        return pltpu.make_async_remote_copy(
            src_ref=ret.at[slot, j], dst_ref=back.at[2 * chip + core], send_sem=ret_send.at[slot, j], recv_sem=ret_recv.at[2 * chip + core],
            device_id={"member": 2 * owners[slot - 1] + j}, device_id_type=MESH,
        )

    slots = [[(link, s) for s in range(STEPS) if s < 4 or link == 0] for link in range(3)]
    slots.append([(link, s) for link in (1, 2) for s in (4, 5)])
    for slot in (4, 1, 2, 3):
        for link, s in slots[slot - 1]:
            guarded(held(link, s), lambda link=link, s=s, slot=slot: finish(bases[link] + s, slot, line_of(link, s)[1]))
        for j in range(2):
            give(slot, j).start()
    for i in range(PER):
        finish(i, 0, i)
    to_sibling = pltpu.make_async_remote_copy(
        src_ref=ret.at[0, 1 - core], dst_ref=back.at[member], send_sem=ret_send.at[0, 0], recv_sem=ret_recv.at[member],
        device_id=sibling, device_id_type=MESH,
    )
    to_sibling.start()

    other_of = lambda c: (c % 4 + 2) % 4 + 4 * (1 - c // 4)
    givers = [
        actual(pick(role, (1, 0, 1, 1))),
        jnp.where(late_pair, actual(pick(role, (5, 5, 5, 2))), other_of(actual(pick(role, (1, 0, 0, 0))))),
        other_of(actual(pick(role, (2, 2, 0, 0)))),
        other_of(actual(pick(role, (5, 5, 5, 2)))),
    ]

    def take(source):
        return pltpu.make_async_remote_copy(
            src_ref=back.at[source], dst_ref=back.at[source], send_sem=ret_send.at[0, 1], recv_sem=ret_recv.at[source],
            device_id=sibling, device_id_type=MESH,
        )

    take(2 * chip + 1 - core).wait_recv()
    for giver in givers:
        for j in range(2):
            take(2 * giver + j).wait_recv()
    computes = lambda c: (c // 4) if c != 3 and c != 5 else 1 - c // 4
    for c in range(2):
        best = jnp.maximum(jnp.full((8, UNIT), -1.0, jnp.float32), jnp.where(mine == c, ret[0, core], -1.0))
        for source in range(16):
            if computes(source // 2) == c:
                best = jnp.maximum(best, back[source])
        for i in range(PER):
            out[c : c + 1, i * UNIT : (i + 1) * UNIT] = jnp.where(own_live[c * PER + i], best[i : i + 1], -1.0)

    with_sibling(core).wait_send()
    for link in range(3):
        give_tile(link, 0).wait_send()
        guarded(goes(link, 4), lambda link=link: give_tile(link, 1).wait_send())

    for axis in range(3):
        for i in range(1, 4):
            part(axis, i, False).wait_send()
    for s in range(STEPS):
        for link in range(3):
            guarded(goes(link, s), lambda link=link: outgoing(link, s).wait_send())
    for i in range(PER):
        exchange(i, half).wait_send()
    for s in range(STEPS):
        for link in range(3):
            guarded(held(link, s), lambda link=link: exchange(bases[link] + s, half).wait_send())
    for slot in range(1, 5):
        for j in range(2):
            give(slot, j).wait_send()
    to_sibling.wait_send()


def solution(mesh):
    units = LR + STEPS

    def local(embeddings, order_rank, lengths):
        d = embeddings.shape[-1]
        f32, dma = jnp.float32, pltpu.SemaphoreType.DMA
        return pl.pallas_call(
            kernel,
            out_shape=jax.ShapeDtypeStruct(order_rank.shape, f32),
            in_specs=[
                pl.BlockSpec(memory_space=pl.ANY),
                pl.BlockSpec(memory_space=pl.ANY),
                pl.BlockSpec(memory_space=pl.ANY),
            ],
            out_specs=pl.BlockSpec(memory_space=pltpu.VMEM),
            scratch_shapes=[
                pltpu.SMEM(lengths.shape, jnp.int32),
                pltpu.VMEM(order_rank.shape, jnp.int32),
                pltpu.VMEM((OTHER + PER, UNIT, d), jnp.bfloat16),
                pltpu.VMEM((units, 2 * UNIT, d), jnp.bfloat16),
                pltpu.VMEM((units, 1, 2 * UNIT), f32),
                pltpu.VMEM((units, UNIT, UNIT), f32),
                pltpu.VMEM((units, UNIT, UNIT), f32),
                pltpu.VMEM((units, 8, 2 * UNIT), f32),
                pltpu.VMEM((2, 24, UNIT), f32),
                pltpu.VMEM((3, 4, 16, UNIT), f32),
                pltpu.VMEM((8, 8, UNIT), f32),
                pltpu.VMEM((5, 2, 8, UNIT), f32),
                pltpu.VMEM((16, 8, UNIT), f32),
                pltpu.VMEM((1, d), f32),
                dma((4,)),
                dma((3, STEPS)),
                dma((3 * STEPS,)),
                dma((units,)),
                dma((units,)),
                dma((1,)),
                dma((1,)),
                dma((3, 4)),
                dma((3, 4)),
                dma((3, 2)),
                dma((8,)),
                dma((5, 2)),
                dma((16,)),
            ],
            compiler_params=pltpu.CompilerParams(collective_id=0, has_side_effects=True, vmem_limit_bytes=60 * 1024 * 1024),
            cost_estimate=pl.CostEstimate(flops=10_000_000_000, bytes_accessed=4_000_000, transcendentals=10_000),
        )(lengths, embeddings.reshape(2, PER, UNIT, d), order_rank)

    placed = (P("group", "member", None), P("group", "member"), P("group"))
    return jax.shard_map(local, mesh=mesh, in_specs=placed, out_specs=P("group", "member"), check_vma=False)
```
